32 devices in a mesh: fsdp: 2 (over x), tile: 8 (over z, core), scan: 2 (over y).
Axes of the slice: x: 2, y: 2, z: 4, core: 2. Of those that a mesh axis runs over, the one named last changes fastest.
Arguments:
- acts: bfloat16 [2, 2, 16, 16, 64, 512], P('scan', 'fsdp', None, 'tile'), may hold values from -6 to 6
- spatial_weight: bfloat16 [9, 512, 512], P(None, None, 'fsdp'), may hold values from -0.09375 to 0.09375
- temporal_weight: bfloat16 [3, 512, 512], P(None, None, 'fsdp'), may hold values from -0.15625 to 0.15625
- readout_weight: bfloat16 [2, 1024, 512], P('scan', 'tile'), may hold values from -0.25 to 0.25
- readout_bias: bfloat16 [2, 1024], P('scan', 'tile'), may hold values from -1.5 to 0.5
- tile_of: int32 [2, 1024, 1], P('scan', 'tile'), may hold values from 0 to 7; in each aligned block of 128 rows (0 to 127, 128 to 255, ..., all dimensions but the last counted through in order) at most 40 rows name the same one
- row_of: int32 [2, 1024], P('scan', 'tile'), may hold values from 0 to 1
- column_of: int32 [2, 1024], P('scan', 'tile'), may hold values from 0 to 63
- spikes: int32 [2, 2, 16, 1024], P('scan', 'fsdp', None, 'tile'), may hold values from 0 to 5
Outputs:
- spatial_grad: float32 [9, 512, 512], P(None, None, 'fsdp')
- temporal_grad: float32 [3, 512, 512], P(None, None, 'fsdp')
- readout_grad: float32 [2, 1024, 512], P('scan', 'tile')
- bias_grad: float32 [2, 1024], P('scan', 'tile')
The draws below stay inside these ranges and needn't reach their ends.
Inputs may be any that keep to these rules, and one draw needn't show every extreme that they name: `tile_of`: among the 128 neurons of one index of tile (aligned blocks of a scan's neurons), at most 40 read one tile.
All inputs are finite; a program needn't handle non-finite values.
Results may differ from the reference program's by a relative error of at most 0.006.
Values may be sent and summed in bfloat16 or wider, within the bound.
A program may use at most 192 MiB of HBM per device.

```python
import math
import jax
import jax.numpy as jnp
import numpy as np
from jax import lax

C = 512
W = 64
FRAMES = 16
ROWS_DEV = 2
NEU_DEV = 128
SCANS = 2
REPS = 2
H = 16
NEU = 1024
CAP = 40
N_TILE = 8


def set_ends(result, own_key, smallest, top_value):
    index_at = [jax.random.randint(jax.random.fold_in(own_key, axis), (), 0, length) for axis, length in enumerate(result.shape)]
    widest = result.shape.index(max(result.shape))
    beside = index_at[:widest] + [(index_at[widest] + 1) % result.shape[widest]] + index_at[widest + 1:]
    return result.at[tuple(index_at)].set(smallest).at[tuple(beside)].set(top_value)


def steps_of(own_key, shape, cuts, least, top_value):
    def one(position, blocks):
        heights = jax.random.uniform(jax.random.fold_in(jax.random.fold_in(own_key, 6), position), (blocks,), jnp.float32, least / len(cuts), top_value / len(cuts))
        return jnp.repeat(jnp.exp(heights), shape[position] // blocks).reshape((-1,) + (1,) * (len(shape) - position - 1))

    factor_of = one(*cuts[0])
    for cut in cuts[1:]:
        factor_of = factor_of * one(*cut)
    return factor_of


def shared_out(rng, own, number, rows, number_of, top, limit, lean):
    sequence = jax.random.permutation(rng, number_of)
    crowded, ordinary = portions_of(number_of, rows * top, limit, lean, True), portions_of(number_of, rows * top, limit, lean, False)
    places = jnp.arange(number_of)

    def named(lengths, offset_by):
        used = int((lengths > 0).sum())
        fixed = max(1, used // 4)
        moved = fixed + (places - fixed + offset_by * (used - fixed)) % max(1, number_of - fixed)
        return jnp.zeros((number_of,), jnp.int32).at[sequence[jnp.where(places < fixed, places, moved)]].set(jnp.asarray(lengths, jnp.int32))

    lengths = jnp.where(number % 4 == 0, named(crowded, number // 4), named(ordinary, number - number // 4 - 1))
    mixed = jax.random.permutation(jax.random.fold_in(own, 3), number_of)
    giver, sink = mixed[0:number_of // 2 * 2:2], mixed[1:number_of // 2 * 2:2]
    room = jnp.minimum(lengths[giver] - 1, limit - lengths[sink]) // 2
    room = jnp.where((giver == sequence[0]) | (sink == sequence[0]) | (lengths[sink] == 0), 0, jnp.maximum(room, 0))
    moved = jax.random.randint(jax.random.fold_in(own, 4), (number_of // 2,), 0, 1 << 20) % (room + 1)
    lengths = lengths.at[giver].add(-moved).at[sink].add(moved)
    items = jnp.searchsorted(jnp.cumsum(lengths), jnp.arange(rows * top), side="right").astype(jnp.int32)
    table = items.reshape(top, rows).T
    table = table[jax.random.permutation(jax.random.fold_in(own, 1), rows)]
    offset_by = jax.random.randint(jax.random.fold_in(own, 2), (rows, 1), 0, top)
    return jnp.take_along_axis(table, (jnp.arange(top)[None, :] + offset_by) % top, axis=1)


def portions_of(number_of, total, bound, skew, full):
    portions = [(1 << 20) // math.isqrt(standing ** skew) + 1 for standing in range(1, number_of + 1)]
    largest = bound if full else min(bound, max(-(-total // number_of), total * portions[0] // sum(portions)))
    least = 1 if total - largest >= number_of - 1 else 0
    holding, rest = [largest] + [least] * (number_of - 1), total - largest - least * (number_of - 1)
    while rest > 0:
        candidates = [i for i in range(1, number_of) if holding[i] < largest] or [i for i in range(1, number_of) if holding[i] < bound]
        mass, remaining = sum([portions[i] for i in candidates]), rest
        for i in candidates:
            extra = min(bound - holding[i], max(1, remaining * portions[i] // mass), rest)
            holding[i] = holding[i] + extra
            rest = rest - extra
    return np.array(holding)


def normal_values(key, dims, deviation, limit, split=(), kind=jnp.bfloat16):
    factor_of = steps_of(key, dims, split, -0.22, 0.18) if split else 1.0
    drawn = jax.random.normal(key, dims, jnp.float32) * deviation * factor_of
    return jnp.minimum(jnp.maximum(drawn, -limit), limit).astype(kind)


def setup_inputs(seed: int = 0) -> dict:
    keys = jax.random.split(jax.random.key(seed), 10)
    acts = normal_values(keys[0], (SCANS, REPS, FRAMES, H, W, C), 1.0, 6.0, ((0, 2), (1, 2), (3, 8)))
    spatial_weight = normal_values(keys[1], (9, C, C), (9 * C) ** -0.5, 0.09375, ((2, 2),))
    temporal_weight = normal_values(keys[2], (3, C, C), (3 * C) ** -0.5, 0.15625, ((2, 2),))
    readout_weight = normal_values(keys[3], (SCANS, NEU, C), C ** -0.5, 0.25, ((0, 2), (1, 8)))
    readout_bias = jnp.clip(-1.5 + 2.0 * jax.random.uniform(keys[4], (SCANS, NEU), jnp.float32) ** steps_of(keys[4], (SCANS, NEU), ((0, 2), (1, 8)), -0.2, 0.2), -1.5, 0.5).astype(jnp.bfloat16)
    tile_of_keys = jax.random.split(jax.random.fold_in(keys[5], 1), SCANS * NEU // NEU_DEV)
    tile_of_turns = jax.random.permutation(jax.random.fold_in(keys[5], 3), SCANS * NEU // NEU_DEV)
    tile_of = jax.vmap(lambda own, number: shared_out(jax.random.fold_in(keys[5], 2), own, number, NEU_DEV, N_TILE, 1, CAP, 2))(tile_of_keys, tile_of_turns).reshape((SCANS, NEU, 1))
    row_of = set_ends(jax.random.randint(keys[6], (SCANS, NEU), 0, ROWS_DEV), jax.random.fold_in(keys[6], 1), 0, ROWS_DEV - 1).astype(jnp.int32)
    column_of = set_ends(jax.random.randint(keys[7], (SCANS, NEU), 0, W), jax.random.fold_in(keys[7], 1), 0, W - 1).astype(jnp.int32)
    spikes = set_ends(jax.random.randint(keys[8], (SCANS, REPS, FRAMES, NEU), 0, 6), jax.random.fold_in(keys[8], 1), 0, 5).astype(jnp.int32)
    return dict(acts=acts, spatial_weight=spatial_weight, temporal_weight=temporal_weight, readout_weight=readout_weight, readout_bias=readout_bias, tile_of=tile_of, row_of=row_of, column_of=column_of, spikes=spikes)


def hold_bf16(values):
    return lax.optimization_barrier(values.astype(jnp.bfloat16)).astype(jnp.float32)


def reference(acts, spatial_weight, temporal_weight, readout_weight, readout_bias, tile_of, row_of, column_of, spikes):
    spatial = spatial_weight.astype(jnp.float32)
    temporal = temporal_weight.astype(jnp.float32)
    spatial_grad = jnp.zeros((9, C, C), jnp.float32)
    temporal_grad = jnp.zeros((3, C, C), jnp.float32)
    readout_list = []
    bias_list = []
    scale_factor = 1.0 / (REPS * FRAMES)
    for scan_index in range(SCANS):
        rows_global = (tile_of[scan_index, :, 0] * ROWS_DEV + row_of[scan_index]).astype(jnp.int32)
        columns = column_of[scan_index].astype(jnp.int32)
        weights_now = readout_weight[scan_index].astype(jnp.float32)
        bias_now = readout_bias[scan_index].astype(jnp.float32)
        weight_acc = jnp.zeros((NEU, C), jnp.float32)
        bias_acc = jnp.zeros((NEU,), jnp.float32)
        for clip_index in range(REPS):
            frames_in = acts[scan_index, clip_index].astype(jnp.float32)
            padded = jnp.pad(frames_in, ((0, 0), (1, 1), (1, 1), (0, 0)))
            spatial_out = jnp.zeros((FRAMES, H, W, C), jnp.float32)
            for tap in range(9):
                row_tap = tap // 3
                col_tap = tap % 3
                spatial_out = spatial_out + jnp.einsum('fhwc,cd->fhwd', padded[:, row_tap:row_tap + H, col_tap:col_tap + W, :], spatial[tap])
            spatial_out = hold_bf16(spatial_out)
            causal = jnp.pad(spatial_out, ((2, 0), (0, 0), (0, 0), (0, 0)))
            mixed = jnp.zeros((FRAMES, H, W, C), jnp.float32)
            for lag in range(3):
                mixed = mixed + jnp.einsum('fhwc,cd->fhwd', causal[2 - lag:2 - lag + FRAMES], temporal[lag])
            features = hold_bf16(jax.nn.elu(mixed))
            picked = features[:, rows_global, columns, :]
            logits = jnp.einsum('fnc,nc->fn', picked, weights_now) + bias_now[None, :]
            delta = (jnp.exp(logits) - spikes[scan_index, clip_index].astype(jnp.float32)) * scale_factor
            weight_acc = weight_acc + jnp.einsum('fn,fnc->nc', delta, picked)
            bias_acc = bias_acc + jnp.sum(delta, axis=0)
            terms = hold_bf16(delta[:, :, None] * weights_now[None, :, :])
            feature_grad = jnp.zeros((FRAMES, H, W, C), jnp.float32).at[:, rows_global, columns, :].add(terms)
            slope = jnp.where(mixed > 0, 1.0, jnp.exp(jnp.minimum(mixed, 0.0)))
            mixed_grad = hold_bf16(feature_grad * slope)
            for lag in range(3):
                temporal_grad = temporal_grad.at[lag].add(jnp.einsum('fhwc,fhwd->cd', causal[2 - lag:2 - lag + FRAMES], mixed_grad))
            back_pad = jnp.pad(mixed_grad, ((0, 2), (0, 0), (0, 0), (0, 0)))
            spatial_back = jnp.zeros((FRAMES, H, W, C), jnp.float32)
            for lag in range(3):
                spatial_back = spatial_back + jnp.einsum('fhwd,cd->fhwc', back_pad[lag:lag + FRAMES], temporal[lag])
            spatial_back = hold_bf16(spatial_back)
            for tap in range(9):
                row_tap = tap // 3
                col_tap = tap % 3
                spatial_grad = spatial_grad.at[tap].add(jnp.einsum('fhwc,fhwd->cd', padded[:, row_tap:row_tap + H, col_tap:col_tap + W, :], spatial_back))
        readout_list.append(weight_acc)
        bias_list.append(bias_acc)
    return spatial_grad, temporal_grad, jnp.stack(readout_list), jnp.stack(bias_list)
```

```python
import jax
import jax.numpy as jnp
from jax import lax
from jax.sharding import PartitionSpec as P

F32 = jnp.float32
BF16 = jnp.bfloat16


def halo_rows(block, axis, dim):
    count = lax.axis_size(axis)
    forward = [(i, i + 1) for i in range(count - 1)]
    backward = [(target, source) for source, target in forward]
    low = lax.ppermute(lax.slice_in_dim(block, block.shape[dim] - 1, None, axis=dim), axis, forward)
    high = lax.ppermute(lax.slice_in_dim(block, 0, 1, axis=dim), axis, backward)
    return low, high


def contract_rows(left, right):
    return lax.dot_general(left, right, (((0,), (0,)), ((), ())), preferred_element_type=F32)


def three_columns(block):
    padded = jnp.pad(block, ((0, 0), (0, 0), (1, 1), (0, 0)))
    width = block.shape[2]
    return jnp.concatenate([padded[:, :, b : b + width] for b in range(3)], axis=-1)


def on_device(
    acts,
    spatial_weight,
    temporal_weight,
    readout_weight,
    readout_bias,
    tile_of,
    row_of,
    column_of,
    spikes,
):
    frames_in = acts[0, 0]
    frames, rows, width, channels = frames_in.shape
    cells = rows * width
    neurons = readout_weight.shape[1]
    rep_count = lax.axis_size("fsdp")
    me = lax.axis_index("tile")

    small = jnp.concatenate(
        [
            spikes[0, 0].T.astype(BF16),
            readout_bias[0][:, None],
            tile_of[0].astype(BF16),
            row_of[0][:, None].astype(BF16),
            column_of[0][:, None].astype(BF16),
        ],
        axis=1,
    )
    small = jnp.pad(small, ((0, 0), (0, -small.shape[1] % 128)))
    table = lax.all_gather(
        jnp.concatenate([readout_weight[0], small], axis=1), "tile", axis=0, tiled=True
    )
    spatial = lax.all_gather(spatial_weight, "fsdp", axis=2, tiled=True)
    temporal = lax.all_gather(temporal_weight, "fsdp", axis=2, tiled=True)
    low, high = halo_rows(frames_in, "tile", 1)
    columns = three_columns(jnp.concatenate([low, frames_in, high], axis=1))

    def patch(a):
        return columns[:, a : a + rows].reshape(-1, 3 * channels)

    taps = spatial.reshape(3, 3 * channels, channels)
    spatial_sum = jnp.dot(patch(0), taps[0], preferred_element_type=F32)
    for a in (1, 2):
        spatial_sum = spatial_sum + jnp.dot(patch(a), taps[a], preferred_element_type=F32)
    spatial_out = spatial_sum.astype(BF16).reshape(frames, cells, channels)
    causal = jnp.pad(spatial_out, ((2, 0), (0, 0), (0, 0)))
    causal3 = jnp.concatenate(
        [causal[2 - lag : 2 - lag + frames].reshape(-1, channels) for lag in range(3)], axis=-1
    )
    mixed = jnp.dot(causal3, temporal.reshape(3 * channels, channels), preferred_element_type=F32)
    features = jax.nn.elu(mixed).astype(BF16)

    weights = table[:, :channels]
    rest = table[:, channels:].astype(F32).T
    counts = rest[:frames]
    bias = rest[frames]
    cell_of = ((rest[frames + 1] - me.astype(F32)) * rows + rest[frames + 2]) * width + rest[frames + 3]
    mask = cell_of[None, :] == jnp.arange(cells).astype(F32)[:, None]
    here = (cell_of >= 0) & (cell_of < cells)
    products = lax.dot_general(
        features, weights, (((1,), (1,)), ((), ())), preferred_element_type=F32
    ).reshape(frames, cells, -1)
    logits = jnp.sum(jnp.where(mask[None], products, 0.0), axis=1) + bias[None, :]
    delta = (jnp.exp(logits) - counts) * (1.0 / (rep_count * frames))
    delta = jnp.where(here[None, :], delta, 0.0)
    spread = jnp.where(mask[None], delta[:, None, :], 0.0).astype(BF16).reshape(frames * cells, -1)
    feature_grad = jnp.dot(spread, weights, preferred_element_type=F32)
    weight_grad = contract_rows(spread, features)
    bias_column = jnp.pad(jnp.sum(delta, axis=0)[:, None], ((0, 0), (0, 127)))
    readout = lax.psum_scatter(
        jnp.concatenate([weight_grad, bias_column], axis=1), "tile", scatter_dimension=0, tiled=True
    )
    readout = lax.psum(readout, "fsdp")

    slope = jnp.where(mixed > 0, 1.0, jnp.exp(jnp.minimum(mixed, 0.0)))
    mixed_grad = (feature_grad * slope).astype(BF16)
    temporal_grad = contract_rows(causal3, mixed_grad).reshape(3, channels, channels)
    back_pad = jnp.pad(mixed_grad.reshape(frames, cells, channels), ((0, 2), (0, 0), (0, 0)))
    spatial_back = jnp.zeros((frames * cells, channels), F32)
    for lag in range(3):
        spatial_back = spatial_back + lax.dot_general(
            back_pad[lag : lag + frames].reshape(-1, channels),
            temporal[lag],
            (((1,), (1,)), ((), ())),
            preferred_element_type=F32,
        )
    spatial_back = spatial_back.astype(BF16)
    spatial_grad = jnp.stack([contract_rows(patch(a), spatial_back) for a in range(3)]).reshape(
        9, channels, channels
    )
    total_spatial, total_temporal = reduce_grads(spatial_grad, temporal_grad)
    return (
        total_spatial,
        total_temporal,
        readout[None, :, :channels],
        readout[None, :, channels],
    )


def reduce_grads(spatial_grad, temporal_grad):
    shards = [
        lax.psum_scatter(grad, "fsdp", scatter_dimension=2, tiled=True)
        for grad in (spatial_grad, temporal_grad)
    ]
    return lax.psum(tuple(shards), ("tile", "scan"))


def solution(mesh):
    return jax.shard_map(
        on_device,
        mesh=mesh,
        in_specs=(
            P("scan", "fsdp", None, "tile", None, None),
            P(None, None, "fsdp"),
            P(None, None, "fsdp"),
            P("scan", "tile", None),
            P("scan", "tile"),
            P("scan", "tile", None),
            P("scan", "tile"),
            P("scan", "tile"),
            P("scan", "fsdp", None, "tile"),
        ),
        out_specs=(
            P(None, None, "fsdp"),
            P(None, None, "fsdp"),
            P("scan", "tile", None),
            P("scan", "tile"),
        ),
        check_vma=False,
    )
```

```python
import jax
import jax.numpy as jnp
from jax import lax
from jax.sharding import PartitionSpec as P

F32 = jnp.float32
BF16 = jnp.bfloat16


def halo_rows(block, axis, dim):
    count = lax.axis_size(axis)
    forward = [(i, i + 1) for i in range(count - 1)]
    backward = [(target, source) for source, target in forward]
    low = lax.ppermute(lax.slice_in_dim(block, block.shape[dim] - 1, None, axis=dim), axis, forward)
    high = lax.ppermute(lax.slice_in_dim(block, 0, 1, axis=dim), axis, backward)
    return low, high


def contract_rows(left, right):
    return lax.dot_general(left, right, (((0,), (0,)), ((), ())), preferred_element_type=F32)


def three_columns(block):
    padded = jnp.pad(block, ((0, 0), (0, 0), (1, 1), (0, 0)))
    width = block.shape[2]
    return jnp.concatenate([padded[:, :, b : b + width] for b in range(3)], axis=-1)


def swap(block, axis, bit=0):
    count = lax.axis_size(axis)
    return lax.ppermute(block, axis, [(i, i ^ (1 << bit)) for i in range(count)])


def in_order(position, own, other, dim):
    return jnp.where(
        position == 0,
        jnp.concatenate([own, other], axis=dim),
        jnp.concatenate([other, own], axis=dim),
    )


def whole_weight(weight):
    if lax.axis_size("fsdp") != 2 or lax.axis_size("tile") % 2:
        return lax.all_gather(weight, "fsdp", axis=2, tiled=True)
    core = lax.axis_index("tile") % 2
    half = weight.shape[1] // 2
    mine = jnp.where(core == 0, weight[:, :half], weight[:, half:])
    first = swap(mine, "fsdp")
    other = in_order(core, first, swap(first, "tile"), 1)
    return in_order(lax.axis_index("fsdp"), weight, other, 2)


def halved(total, axis, bit, dim):
    side = (lax.axis_index(axis) >> bit) & 1
    parts = [lax.index_in_dim(total, i, dim, keepdims=False) for i in range(2)]
    sent = jnp.where(side == 0, parts[1], parts[0]).astype(BF16)
    kept = jnp.where(side == 0, parts[0], parts[1])
    return kept + swap(sent, axis, bit).astype(F32)


def reduced(grad):
    taps, channels, out_channels = grad.shape
    scans, tiles = lax.axis_size("scan"), lax.axis_size("tile")
    scan_bits, tile_bits = scans.bit_length() - 1, tiles.bit_length() - 1
    bits = [("scan", b) for b in reversed(range(scan_bits))]
    bits += [("tile", b) for b in reversed(range(tile_bits))]
    total = grad.reshape((taps,) + (2,) * len(bits) + (-1, out_channels))

    def step(total, which):
        total = halved(total, *which, 1 + bits.index(which))
        bits.remove(which)
        return total

    total = step(total, ("tile", 0))
    half = out_channels // 2
    side = lax.axis_index("fsdp")
    left, right = total[..., :half], total[..., half:]
    sent = jnp.where(side == 0, right, left).astype(BF16)
    total = jnp.where(side == 0, left, right) + swap(sent, "fsdp").astype(F32)
    for b in range(scan_bits):
        total = step(total, ("scan", b))
    for b in range(1, tile_bits):
        total = step(total, ("tile", b))
    return lax.all_gather(total.astype(BF16), ("scan", "tile"), axis=1, tiled=True).astype(F32)


def on_device(
    acts,
    spatial_weight,
    temporal_weight,
    readout_weight,
    readout_bias,
    tile_of,
    row_of,
    column_of,
    spikes,
):
    frames_in = acts[0, 0]
    frames, rows, width, channels = frames_in.shape
    cells = rows * width
    neurons = readout_weight.shape[1]
    rep_count = lax.axis_size("fsdp")
    me = lax.axis_index("tile")

    small = jnp.concatenate(
        [
            spikes[0, 0].T.astype(BF16),
            readout_bias[0][:, None],
            tile_of[0].astype(BF16),
            row_of[0][:, None].astype(BF16),
            column_of[0][:, None].astype(BF16),
        ],
        axis=1,
    )
    small = jnp.pad(small, ((0, 0), (0, -small.shape[1] % 128)))
    table = lax.all_gather(
        jnp.concatenate([readout_weight[0], small], axis=1), "tile", axis=0, tiled=True
    )
    spatial = whole_weight(spatial_weight)
    temporal = whole_weight(temporal_weight)
    low, high = halo_rows(frames_in, "tile", 1)
    columns = three_columns(jnp.concatenate([low, frames_in, high], axis=1))

    def patch(a):
        return columns[:, a : a + rows].reshape(-1, 3 * channels)

    taps = spatial.reshape(3, 3 * channels, channels)
    spatial_sum = jnp.dot(patch(0), taps[0], preferred_element_type=F32)
    for a in (1, 2):
        spatial_sum = spatial_sum + jnp.dot(patch(a), taps[a], preferred_element_type=F32)
    spatial_out = spatial_sum.astype(BF16).reshape(frames, cells, channels)
    causal = jnp.pad(spatial_out, ((2, 0), (0, 0), (0, 0)))
    causal3 = jnp.concatenate(
        [causal[2 - lag : 2 - lag + frames].reshape(-1, channels) for lag in range(3)], axis=-1
    )
    mixed = jnp.dot(causal3, temporal.reshape(3 * channels, channels), preferred_element_type=F32)
    features = jax.nn.elu(mixed).astype(BF16)

    weights = table[:, :channels]
    rest = table[:, channels:].astype(F32).T
    counts = rest[:frames]
    bias = rest[frames]
    cell_of = ((rest[frames + 1] - me.astype(F32)) * rows + rest[frames + 2]) * width + rest[frames + 3]
    mask = cell_of[None, :] == jnp.arange(cells).astype(F32)[:, None]
    here = (cell_of >= 0) & (cell_of < cells)
    products = lax.dot_general(
        features, weights, (((1,), (1,)), ((), ())), preferred_element_type=F32
    ).reshape(frames, cells, -1)
    logits = jnp.sum(jnp.where(mask[None], products, 0.0), axis=1) + bias[None, :]
    delta = (jnp.exp(logits) - counts) * (1.0 / (rep_count * frames))
    delta = jnp.where(here[None, :], delta, 0.0)
    spread = jnp.where(mask[None], delta[:, None, :], 0.0).astype(BF16).reshape(frames * cells, -1)
    feature_grad = jnp.dot(spread, weights, preferred_element_type=F32)
    weight_grad = contract_rows(spread, features)
    bias_column = jnp.pad(jnp.sum(delta, axis=0)[:, None], ((0, 0), (0, 127)))
    readout = lax.psum_scatter(
        jnp.concatenate([weight_grad, bias_column], axis=1), "tile", scatter_dimension=0, tiled=True
    )
    readout = readout + swap(readout, "fsdp") if rep_count == 2 else lax.psum(readout, "fsdp")

    slope = jnp.where(mixed > 0, 1.0, jnp.exp(jnp.minimum(mixed, 0.0)))
    mixed_grad = (feature_grad * slope).astype(BF16)
    temporal_grad = contract_rows(causal3, mixed_grad).reshape(3, channels, channels)
    back_pad = jnp.pad(mixed_grad.reshape(frames, cells, channels), ((0, 2), (0, 0), (0, 0)))
    spatial_back = jnp.zeros((frames * cells, channels), F32)
    for lag in range(3):
        spatial_back = spatial_back + lax.dot_general(
            back_pad[lag : lag + frames].reshape(-1, channels),
            temporal[lag],
            (((1,), (1,)), ((), ())),
            preferred_element_type=F32,
        )
    spatial_back = spatial_back.astype(BF16)
    spatial_grads = [
        contract_rows(patch(a), spatial_back).reshape(3, channels, channels) for a in range(3)
    ]
    total_spatial, total_temporal = reduce_grads(spatial_grads, temporal_grad)
    return (
        total_spatial,
        total_temporal,
        readout[None, :, :channels],
        readout[None, :, channels],
    )


def reduce_grads(spatial_grads, temporal_grad):
    sizes = [lax.axis_size(axis) for axis in ("scan", "tile")]
    if lax.axis_size("fsdp") == 2 and not any(size & (size - 1) for size in sizes):
        one = reduced(jnp.concatenate([temporal_grad, spatial_grads[0]]))
        two = reduced(jnp.concatenate(spatial_grads[1:]))
        return jnp.concatenate([one[3:], two]), one[:3]
    shards = [
        lax.psum_scatter(grad, "fsdp", scatter_dimension=2, tiled=True)
        for grad in (jnp.concatenate(spatial_grads), temporal_grad)
    ]
    return lax.psum(tuple(shards), ("tile", "scan"))


def solution(mesh):
    return jax.shard_map(
        on_device,
        mesh=mesh,
        in_specs=(
            P("scan", "fsdp", None, "tile", None, None),
            P(None, None, "fsdp"),
            P(None, None, "fsdp"),
            P("scan", "tile", None),
            P("scan", "tile"),
            P("scan", "tile", None),
            P("scan", "tile"),
            P("scan", "tile"),
            P("scan", "fsdp", None, "tile"),
        ),
        out_specs=(
            P(None, None, "fsdp"),
            P(None, None, "fsdp"),
            P("scan", "tile", None),
            P("scan", "tile"),
        ),
        check_vma=False,
    )
```

```python
import jax
import jax.numpy as jnp
from jax import lax
from jax.sharding import PartitionSpec as P

F32 = jnp.float32
BF16 = jnp.bfloat16


def halo_rows(block, axis, dim):
    count = lax.axis_size(axis)
    forward = [(i, i + 1) for i in range(count - 1)]
    backward = [(target, source) for source, target in forward]
    low = lax.ppermute(lax.slice_in_dim(block, block.shape[dim] - 1, None, axis=dim), axis, forward)
    high = lax.ppermute(lax.slice_in_dim(block, 0, 1, axis=dim), axis, backward)
    return low, high


def contract_rows(left, right):
    return lax.dot_general(left, right, (((0,), (0,)), ((), ())), preferred_element_type=F32)


def three_columns(block):
    padded = jnp.pad(block, ((0, 0), (0, 0), (1, 1), (0, 0)))
    width = block.shape[2]
    return jnp.concatenate([padded[:, :, b : b + width] for b in range(3)], axis=-1)


def swap(block, axis, bit=0):
    count = lax.axis_size(axis)
    return lax.ppermute(block, axis, [(i, i ^ (1 << bit)) for i in range(count)])


def in_order(position, own, other, dim):
    return jnp.where(
        position == 0,
        jnp.concatenate([own, other], axis=dim),
        jnp.concatenate([other, own], axis=dim),
    )


def whole_weight(weight):
    if lax.axis_size("fsdp") != 2 or lax.axis_size("tile") % 2:
        return lax.all_gather(weight, "fsdp", axis=2, tiled=True)
    core = lax.axis_index("tile") % 2
    half = weight.shape[1] // 2
    mine = jnp.where(core == 0, weight[:, :half], weight[:, half:])
    first = swap(mine, "fsdp")
    other = in_order(core, first, swap(first, "tile"), 1)
    return in_order(lax.axis_index("fsdp"), weight, other, 2)


def halved(total, axis, bit, dim):
    side = (lax.axis_index(axis) >> bit) & 1
    parts = [lax.index_in_dim(total, i, dim, keepdims=False) for i in range(2)]
    sent = jnp.where(side == 0, parts[1], parts[0]).astype(BF16)
    kept = jnp.where(side == 0, parts[0], parts[1])
    return kept + swap(sent, axis, bit).astype(F32)


def reduced(grad):
    lanes = grad.shape[1]
    scan_bits = lax.axis_size("scan").bit_length() - 1
    tile_bits = lax.axis_size("tile").bit_length() - 1
    bits = [("fsdp", 0)] + [("scan", b) for b in reversed(range(scan_bits))]
    bits += [("tile", b) for b in reversed(range(tile_bits))]
    total = grad.reshape((2,) * len(bits) + (-1, lanes))
    order = [("tile", 0), ("fsdp", 0)] + [("scan", b) for b in range(scan_bits)]
    for which in order + [("tile", b) for b in range(1, tile_bits)]:
        total = halved(total, *which, bits.index(which))
        bits.remove(which)
    return lax.all_gather(total.astype(BF16), ("scan", "tile"), axis=0, tiled=True)


def on_device(
    acts,
    spatial_weight,
    temporal_weight,
    readout_weight,
    readout_bias,
    tile_of,
    row_of,
    column_of,
    spikes,
):
    rows_in = acts[0, 0].transpose(1, 0, 2, 3)
    rows, frames, width, channels = rows_in.shape
    cells = rows * width
    neurons = readout_weight.shape[1]
    rep_count = lax.axis_size("fsdp")
    me = lax.axis_index("tile")

    small = jnp.concatenate(
        [
            spikes[0, 0].T.astype(BF16),
            readout_bias[0][:, None],
            tile_of[0].astype(BF16),
            row_of[0][:, None].astype(BF16),
            column_of[0][:, None].astype(BF16),
        ],
        axis=1,
    )
    small = jnp.pad(small, ((0, 0), (0, -small.shape[1] % 128)))
    table = lax.all_gather(
        jnp.concatenate([readout_weight[0], small], axis=1), "tile", axis=0, tiled=True
    )
    spatial = whole_weight(spatial_weight)
    temporal = whole_weight(temporal_weight)
    low, high = halo_rows(rows_in, "tile", 0)
    columns = three_columns(jnp.concatenate([low, rows_in, high], axis=0))

    def patch(a):
        return columns[a : a + rows].reshape(-1, 3 * channels)

    taps = spatial.reshape(3, 3 * channels, channels)
    spatial_sum = jnp.dot(patch(0), taps[0], preferred_element_type=F32)
    for a in (1, 2):
        spatial_sum = spatial_sum + jnp.dot(patch(a), taps[a], preferred_element_type=F32)
    spatial_out = spatial_sum.astype(BF16).reshape(rows, frames, width, channels)
    causal = jnp.pad(spatial_out, ((0, 0), (2, 0), (0, 0), (0, 0)))
    causal3 = jnp.concatenate(
        [causal[:, 2 - lag : 2 - lag + frames].reshape(-1, channels) for lag in range(3)], axis=-1
    )
    mixed = jnp.dot(causal3, temporal.reshape(3 * channels, channels), preferred_element_type=F32)
    features = jax.nn.elu(mixed).astype(BF16)

    weights = table[:, :channels]
    rest = table[:, channels:].astype(F32).T
    counts = rest[:frames]
    bias = rest[frames]
    cell_of = ((rest[frames + 1] - me.astype(F32)) * rows + rest[frames + 2]) * width + rest[frames + 3]
    mask = (cell_of[None, :] == jnp.arange(cells).astype(F32)[:, None]).reshape(rows, 1, width, -1)
    here = (cell_of >= 0) & (cell_of < cells)
    products = lax.dot_general(
        features, weights, (((1,), (1,)), ((), ())), preferred_element_type=F32
    ).reshape(rows, frames, width, -1)
    logits = jnp.sum(jnp.where(mask, products, 0.0), axis=(0, 2)) + bias[None, :]
    delta = (jnp.exp(logits) - counts) * (1.0 / (rep_count * frames))
    delta = jnp.where(here[None, :], delta, 0.0)
    spread = jnp.where(mask, delta[None, :, None, :], 0.0).astype(BF16).reshape(frames * cells, -1)
    feature_grad = jnp.dot(spread, weights, preferred_element_type=F32)
    weight_grad = contract_rows(spread, features)
    bias_column = jnp.pad(jnp.sum(delta, axis=0)[:, None], ((0, 0), (0, 127)))
    readout = lax.psum_scatter(
        jnp.concatenate([weight_grad, bias_column], axis=1), "tile", scatter_dimension=0, tiled=True
    )
    readout = readout + swap(readout, "fsdp") if rep_count == 2 else lax.psum(readout, "fsdp")

    slope = jnp.where(mixed > 0, 1.0, jnp.exp(jnp.minimum(mixed, 0.0)))
    mixed_grad = (feature_grad * slope).astype(BF16)
    temporal_grad = contract_rows(mixed_grad, causal3)
    back_pad = jnp.pad(
        mixed_grad.reshape(rows, frames, width, channels), ((0, 0), (0, 2), (0, 0), (0, 0))
    )
    spatial_back = jnp.zeros((frames * cells, channels), F32)
    for lag in range(3):
        spatial_back = spatial_back + lax.dot_general(
            back_pad[:, lag : lag + frames].reshape(-1, channels),
            temporal[lag],
            (((1,), (1,)), ((), ())),
            preferred_element_type=F32,
        )
    spatial_back = spatial_back.astype(BF16)
    spatial_grads = [contract_rows(spatial_back, patch(a)) for a in range(3)]
    total_spatial, total_temporal = reduce_grads(spatial_grads, temporal_grad)
    return (
        total_spatial,
        total_temporal,
        readout[None, :, :channels],
        readout[None, :, channels],
    )


def taps_first(grad, channels):
    return grad.reshape(grad.shape[0], -1, channels).transpose(1, 2, 0).astype(F32)


def reduce_grads(spatial_grads, temporal_grad):
    channels = temporal_grad.shape[0]
    sizes = [lax.axis_size(axis) for axis in ("scan", "tile")]
    if lax.axis_size("fsdp") == 2 and not any(size & (size - 1) for size in sizes):
        pieces = [
            reduced(piece)
            for piece in (
                temporal_grad,
                jnp.concatenate(spatial_grads[:2], axis=1),
                spatial_grads[2],
            )
        ]
    else:
        pieces = [
            lax.psum(
                lax.psum_scatter(piece, "fsdp", scatter_dimension=0, tiled=True), ("tile", "scan")
            )
            for piece in [temporal_grad] + spatial_grads
        ]
    turned = [taps_first(piece, channels) for piece in pieces]
    return jnp.concatenate(turned[1:]), turned[0]


def solution(mesh):
    return jax.shard_map(
        on_device,
        mesh=mesh,
        in_specs=(
            P("scan", "fsdp", None, "tile", None, None),
            P(None, None, "fsdp"),
            P(None, None, "fsdp"),
            P("scan", "tile", None),
            P("scan", "tile"),
            P("scan", "tile", None),
            P("scan", "tile"),
            P("scan", "tile"),
            P("scan", "fsdp", None, "tile"),
        ),
        out_specs=(
            P(None, None, "fsdp"),
            P(None, None, "fsdp"),
            P("scan", "tile", None),
            P("scan", "tile"),
        ),
        check_vma=False,
    )
```

```python
import jax
import jax.numpy as jnp
from jax import lax
from jax.sharding import PartitionSpec as P

F32 = jnp.float32
BF16 = jnp.bfloat16


def halo_rows(block, axis, dim):
    count = lax.axis_size(axis)
    forward = [(i, i + 1) for i in range(count - 1)]
    backward = [(target, source) for source, target in forward]
    low = lax.ppermute(lax.slice_in_dim(block, block.shape[dim] - 1, None, axis=dim), axis, forward)
    high = lax.ppermute(lax.slice_in_dim(block, 0, 1, axis=dim), axis, backward)
    return low, high


def contract_rows(left, right):
    return lax.dot_general(left, right, (((0,), (0,)), ((), ())), preferred_element_type=F32)


def three_columns(block):
    padded = jnp.pad(block, ((0, 0), (0, 0), (1, 1), (0, 0)))
    width = block.shape[2]
    return jnp.concatenate([padded[:, :, b : b + width] for b in range(3)], axis=-1)


def swap(block, axis, bit=0):
    count = lax.axis_size(axis)
    return lax.ppermute(block, axis, [(i, i ^ (1 << bit)) for i in range(count)])


def in_order(position, own, other, dim):
    return jnp.where(
        position == 0,
        jnp.concatenate([own, other], axis=dim),
        jnp.concatenate([other, own], axis=dim),
    )


def whole_weight(weight, beside):
    if lax.axis_size("fsdp") != 2 or lax.axis_size("tile") % 2:
        return lax.all_gather(weight, "fsdp", axis=2, tiled=True), beside
    core = lax.axis_index("tile") % 2
    half = weight.shape[1] // 2
    mine = jnp.where(core == 0, weight[:, :half], weight[:, half:])
    first, beside = lax.optimization_barrier((swap(mine, "fsdp"), beside))
    other = in_order(core, first, swap(first, "tile"), 1)
    return in_order(lax.axis_index("fsdp"), weight, other, 2), beside


def halved(total, axis, bit, dim):
    side = (lax.axis_index(axis) >> bit) & 1
    parts = [lax.index_in_dim(total, i, dim, keepdims=False) for i in range(2)]
    sent = jnp.where(side == 0, parts[1], parts[0]).astype(BF16)
    kept = jnp.where(side == 0, parts[0], parts[1])
    return kept + swap(sent, axis, bit).astype(F32)


def reduced(grad):
    lanes = grad.shape[1]
    scan_bits = lax.axis_size("scan").bit_length() - 1
    tile_bits = lax.axis_size("tile").bit_length() - 1
    bits = [("fsdp", 0)] + [("scan", b) for b in reversed(range(scan_bits))]
    bits += [("tile", b) for b in reversed(range(tile_bits))]
    total = grad.reshape((2,) * len(bits) + (-1, lanes))
    order = [("tile", 0), ("fsdp", 0)] + [("scan", b) for b in range(scan_bits)]
    for which in order + [("tile", b) for b in range(1, tile_bits)]:
        total = halved(total, *which, bits.index(which))
        bits.remove(which)
    return total.astype(BF16)


def gathered(shard):
    return lax.all_gather(shard, ("scan", "tile"), axis=0, tiled=True)


def on_device(
    acts,
    spatial_weight,
    temporal_weight,
    readout_weight,
    readout_bias,
    tile_of,
    row_of,
    column_of,
    spikes,
):
    rows_in = acts[0, 0].transpose(1, 0, 2, 3)
    rows, frames, width, channels = rows_in.shape
    cells = rows * width
    neurons = readout_weight.shape[1]
    rep_count = lax.axis_size("fsdp")
    me = lax.axis_index("tile")

    small = jnp.concatenate(
        [
            spikes[0, 0].T.astype(BF16),
            readout_bias[0][:, None],
            tile_of[0].astype(BF16),
            row_of[0][:, None].astype(BF16),
            column_of[0][:, None].astype(BF16),
        ],
        axis=1,
    )
    small = jnp.pad(small, ((0, 0), (0, -small.shape[1] % 128)))
    table = lax.all_gather(
        jnp.concatenate([readout_weight[0], small], axis=1), "tile", axis=0, tiled=True
    )
    low, high = halo_rows(rows_in, "tile", 0)
    columns = three_columns(jnp.concatenate([low, rows_in, high], axis=0))
    spatial, columns = whole_weight(spatial_weight, columns)
    temporal, _ = whole_weight(temporal_weight, ())

    def patch(a):
        return columns[a : a + rows].reshape(-1, 3 * channels)

    taps = spatial.reshape(3, 3 * channels, channels)
    spatial_sum = jnp.dot(patch(0), taps[0], preferred_element_type=F32)
    for a in (1, 2):
        spatial_sum = spatial_sum + jnp.dot(patch(a), taps[a], preferred_element_type=F32)
    spatial_out = spatial_sum.astype(BF16).reshape(rows, frames, width, channels)
    causal = jnp.pad(spatial_out, ((0, 0), (2, 0), (0, 0), (0, 0)))
    causal3 = jnp.concatenate(
        [causal[:, 2 - lag : 2 - lag + frames].reshape(-1, channels) for lag in range(3)], axis=-1
    )
    mixed = jnp.dot(causal3, temporal.reshape(3 * channels, channels), preferred_element_type=F32)
    features = jax.nn.elu(mixed).astype(BF16)

    weights = table[:, :channels]
    rest = table[:, channels:].astype(F32).T
    counts = rest[:frames]
    bias = rest[frames]
    cell_of = ((rest[frames + 1] - me.astype(F32)) * rows + rest[frames + 2]) * width + rest[frames + 3]
    mask = (cell_of[None, :] == jnp.arange(cells).astype(F32)[:, None]).reshape(rows, 1, width, -1)
    here = (cell_of >= 0) & (cell_of < cells)
    products = lax.dot_general(
        features, weights, (((1,), (1,)), ((), ())), preferred_element_type=F32
    ).reshape(rows, frames, width, -1)
    logits = jnp.sum(jnp.where(mask, products, 0.0), axis=(0, 2)) + bias[None, :]
    delta = (jnp.exp(logits) - counts) * (1.0 / (rep_count * frames))
    delta = jnp.where(here[None, :], delta, 0.0)
    spread = jnp.where(mask, delta[None, :, None, :], 0.0).astype(BF16).reshape(frames * cells, -1)
    feature_grad = jnp.dot(spread, weights, preferred_element_type=F32)
    weight_grad = contract_rows(spread, features)
    bias_column = jnp.pad(jnp.sum(delta, axis=0)[:, None], ((0, 0), (0, 127)))
    readout = lax.psum_scatter(
        jnp.concatenate([weight_grad, bias_column], axis=1), "tile", scatter_dimension=0, tiled=True
    )
    readout = readout + swap(readout, "fsdp") if rep_count == 2 else lax.psum(readout, "fsdp")

    slope = jnp.where(mixed > 0, 1.0, jnp.exp(jnp.minimum(mixed, 0.0)))
    mixed_grad = (feature_grad * slope).astype(BF16)
    temporal_grad = contract_rows(mixed_grad, causal3)
    back_pad = jnp.pad(
        mixed_grad.reshape(rows, frames, width, channels), ((0, 0), (0, 2), (0, 0), (0, 0))
    )
    spatial_back = jnp.zeros((frames * cells, channels), F32)
    for lag in range(3):
        spatial_back = spatial_back + lax.dot_general(
            back_pad[:, lag : lag + frames].reshape(-1, channels),
            temporal[lag],
            (((1,), (1,)), ((), ())),
            preferred_element_type=F32,
        )
    spatial_back = spatial_back.astype(BF16)
    spatial_grads = [contract_rows(spatial_back, patch(a)) for a in range(3)]
    total_spatial, total_temporal = reduce_grads(spatial_grads, temporal_grad)
    return (
        total_spatial,
        total_temporal,
        readout[None, :, :channels],
        readout[None, :, channels],
    )


def taps_first(grad, channels):
    return grad.reshape(grad.shape[0], -1, channels).transpose(1, 2, 0).astype(F32)


def reduce_grads(spatial_grads, temporal_grad):
    channels = temporal_grad.shape[0]
    sizes = [lax.axis_size(axis) for axis in ("scan", "tile")]
    if lax.axis_size("fsdp") == 2 and not any(size & (size - 1) for size in sizes):
        spatial = [reduced(jnp.concatenate(spatial_grads[:2], axis=1)), reduced(spatial_grads[2])]
        pieces = [gathered(reduced(temporal_grad)), gathered(jnp.concatenate(spatial, axis=1))]
    else:
        pieces = [
            lax.psum(
                lax.psum_scatter(piece, "fsdp", scatter_dimension=0, tiled=True), ("tile", "scan")
            )
            for piece in [temporal_grad] + spatial_grads
        ]
    turned = [taps_first(piece, channels) for piece in pieces]
    return jnp.concatenate(turned[1:]), turned[0]


def solution(mesh):
    return jax.shard_map(
        on_device,
        mesh=mesh,
        in_specs=(
            P("scan", "fsdp", None, "tile", None, None),
            P(None, None, "fsdp"),
            P(None, None, "fsdp"),
            P("scan", "tile", None),
            P("scan", "tile"),
            P("scan", "tile", None),
            P("scan", "tile"),
            P("scan", "tile"),
            P("scan", "fsdp", None, "tile"),
        ),
        out_specs=(
            P(None, None, "fsdp"),
            P(None, None, "fsdp"),
            P("scan", "tile", None),
            P("scan", "tile"),
        ),
        check_vma=False,
    )
```
